32 devices in a mesh: group: 2 (over y), chan: 4 (over z), tm: 4 (over x, core).
Axes of the slice: x: 2, y: 2, z: 4, core: 2. Of those that a mesh axis runs over, the one named last changes fastest.
Arguments:
- samples: bfloat16 [8192, 1024], P(('group', 'tm'), 'chan'), parts along dimension 0, may hold values from -6 to 6
- pair_mask: int32 [8, 4], P(('group', 'chan')), parts along dimension 0, may hold values 0 or 1
Outputs:
- cross_cov: float32 [32, 2048, 1024], P('tm', ('group', 'chan')), parts along dimension 1
The draws below stay inside these ranges and needn't reach their ends.
There are 2 independent parts, one for each index of `group`. The reference program is written for one: setup_inputs(seed, part) draws one part's arguments, and reference() takes and returns one part's arrays. A program takes and returns all parts, laid end to end along the dimension named above; each array names one. Nothing has to cross between parts.
All inputs are finite; a program needn't handle non-finite values. No bound on the sum of `pair_mask` on one device may be relied on, other than what follows from the above.
Results may differ from the reference program's by a relative error of at most 0.0003.
Values may be sent and summed in bfloat16 or wider, within the bound.
A program may use at most 128 MiB of HBM per device.

```python
import jax
import jax.numpy as jnp
from jax import lax

B = 256
LAGS = 32
STEPS = 4
CHANNELS = 1024
TIME = 4096
N_CHAN = 4


def plant(entries, own_key, smallest, largest):
    place = [jax.random.randint(jax.random.fold_in(own_key, axis), (), 0, length) for axis, length in enumerate(entries.shape)]
    main_axis = entries.shape.index(max(entries.shape))
    neighbour = place[:main_axis] + [(place[main_axis] + 1) % entries.shape[main_axis]] + place[main_axis + 1:]
    return entries.at[tuple(place)].set(smallest).at[tuple(neighbour)].set(largest)


def block_levels(rng, extent, shards, least, top_value):
    def one(axis_at, blocks):
        steps = jax.random.uniform(jax.random.fold_in(jax.random.fold_in(rng, 6), axis_at), (blocks,), jnp.float32, least / len(shards), top_value / len(shards))
        return jnp.repeat(jnp.exp(steps), extent[axis_at] // blocks).reshape((-1,) + (1,) * (len(extent) - axis_at - 1))

    gain = one(*shards[0])
    for cut in shards[1:]:
        gain = gain * one(*cut)
    return gain


def normal_values(stream_key, shape, deviation, most, split=(), kind=jnp.bfloat16):
    gain = block_levels(stream_key, shape, split, -0.22, 0.18) if split else 1.0
    drawn = jax.random.normal(stream_key, shape, jnp.float32) * deviation * gain
    return jnp.minimum(jnp.maximum(drawn, -most), most).astype(kind)


def setup_inputs(seed: int = 0, part: int = 0) -> dict:
    streams_of = jax.random.split(jax.random.key(seed), 3)
    own_keys = jax.random.split(jax.random.fold_in(streams_of[2], part), 3)
    samples = normal_values(own_keys[0], (TIME, CHANNELS), 1.0, 6.0, ((0, 4), (1, 4)))
    pair_mask = plant((jax.random.randint(own_keys[1], (N_CHAN, STEPS), 0, 4) < 3).astype(jnp.int32), jax.random.fold_in(own_keys[1], 1), 0, 1)
    return dict(samples=samples, pair_mask=pair_mask)


def reference(samples, pair_mask):
    blocks = CHANNELS // B
    widened = samples.astype(jnp.float32)
    padded = jnp.concatenate([widened, jnp.zeros((LAGS, CHANNELS), jnp.float32)], axis=0)

    def one_block(index):
        columns = lax.dynamic_slice_in_dim(padded, index * B, B, 1)
        stacked = jnp.concatenate([lax.dynamic_slice_in_dim(columns, j, TIME, 0) for j in range(LAGS)], axis=1)
        pieces = []
        for step in range(STEPS):
            other = ((index + step) % blocks).astype(jnp.int32)
            partner = lax.dynamic_slice_in_dim(widened, other * B, B, 1)
            product = lax.dot_general(stacked, partner, (((0,), (0,)), ((), ())), precision=lax.Precision.HIGHEST, preferred_element_type=jnp.float32)
            flag = pair_mask[index, step].astype(jnp.float32)
            pieces.append(product.reshape(LAGS, B, B) * flag)
        return jnp.concatenate(pieces, axis=2)
    stacked_all = lax.map(one_block, jnp.arange(blocks, dtype=jnp.int32))
    raw = jnp.transpose(stacked_all, (1, 0, 2, 3)).reshape(LAGS, CHANNELS, STEPS * B)
    return raw / jnp.sqrt(jnp.float32(TIME))
```

```python
import functools

import jax
import jax.numpy as jnp
from jax import lax
from jax.experimental import pallas as pl
from jax.experimental.pallas import tpu as pltpu
from jax.sharding import PartitionSpec as P

LAGS = 32
STEPS = 4
PIECES = 2


def from_behind(value, axis, steps):
    count = lax.axis_size(axis)
    pairs = [(source, (source + steps) % count) for source in range(count)]
    return lax.ppermute(value, axis, pairs)


def cycle_partners(block):
    partners = [block]
    moving = block
    for step in range(1, STEPS):
        moving = from_behind(moving, "chan", -1)
        partners.append(moving)
    return partners


def lagged_product(stacked, partner, flag, count, width):

    def compute():
        product = lax.dot_general(
            stacked, partner, (((0,), (0,)), ((), ())), preferred_element_type=jnp.float32
        )
        return product.reshape(count, width, width)

    def nothing():
        return jnp.zeros((count, width, width), jnp.float32)

    return lax.cond(flag > 0, compute, nothing)


def shards(samples, pair_mask):
    width = samples.shape[1]
    slabs = lax.axis_size("tm")
    lag_dev = LAGS // slabs
    flags = pair_mask[0]
    time_total = samples.shape[0] * slabs
    series = lax.all_gather(samples, "tm", axis=0, tiled=True)
    partners = cycle_partners(series)
    length = series.shape[0]
    first = lax.axis_index("tm") * lag_dev
    padded = jnp.concatenate([series, jnp.zeros((LAGS, width), series.dtype)], axis=0)
    stacked = jnp.concatenate(
        [lax.dynamic_slice_in_dim(padded, first + j, length, 0) for j in range(lag_dev)], axis=1
    )
    raw = jnp.concatenate(
        [
            lagged_product(stacked, partners[step], flags[step], lag_dev, width)
            for step in range(STEPS)
        ],
        axis=2,
    )
    return raw / jnp.sqrt(jnp.float32(time_total))


def kernel(slab, width, lags, flags, own, out, got, wide, stack, total,
           own_sem, out_sem, send_sem, recv_sem):
    z = lax.axis_index("chan")
    m = lax.axis_index("tm")
    x, core = m // 2, m % 2
    other = 1 - x
    last = STEPS - 1
    end = (z == 0) | (z == last)
    mid = (z > 0) & (z < last)
    twin = z + 1 - 2 * (z % 2)
    sibling = {"tm": 2 * x + 1 - core}
    across = {"tm": 2 * other + core}
    up, down = {"chan": z + 1}, {"chan": z - 1}
    rows = slab // PIECES
    length = 4 * slab
    factor = 1.0 / (float(length) ** 0.5)
    high = z // 2
    low = z % 2
    near = 1 + low
    far = 3 * (1 - high)
    middle = 6 - z - near - far
    sent = []

    def home(zp, xp, plane, h, count=1):
        begin = pl.multiple_of((2 * xp + plane) * slab + h * rows, rows)
        return got.at[zp, pl.ds(begin, count * rows), :]

    def send(cond, way, target, zp, xp, h):
        piece = home(zp, xp, core, h)
        copy = pltpu.make_async_remote_copy(
            src_ref=piece,
            dst_ref=piece,
            send_sem=send_sem.at[way, zp, xp, h],
            recv_sem=recv_sem.at[zp, 2 * xp + core, h],
            device_id=target,
            device_id_type=pl.DeviceIdType.MESH,
        )
        if cond is None:
            copy.start()
        else:
            pl.when(cond)(copy.start)
        return cond, copy

    def arrive(zp, xp, plane, h):
        piece = home(zp, xp, plane, h)
        pltpu.make_async_copy(piece, piece, recv_sem.at[zp, 2 * xp + plane, h]).wait()

    def from_z(r, h):
        for d in (1, -1):
            zp = z + d * r
            here = (zp >= 0) & (zp <= last)
            zq = jnp.clip(zp, 0, last)

            @pl.when(here)
            def _():
                arrive(zq, x, core, h)

            onward = (z > 0) if d == 1 else (z < last)
            sent.append(send(here & onward, 0 if d == 1 else 1, down if d == 1 else up, zq, x, h))
            skip = (zp == twin) if h >= PIECES // 2 else ((zp == twin) & mid)
            sent.append(send(here & jnp.logical_not(skip), 2, across, zq, x, h))
            sent.append(send(here, 3, sibling, zq, x, h))

    def lend(h, cond):
        sent.append(send(cond & (low == 0), 1, up, z, other, h))
        sent.append(send(cond & (low == 1), 0, down, z, other, h))

    def from_x(zp, h):
        arrive(zp, other, core, h)
        sent.append(send(None, 3, sibling, zp, other, h))

    def from_sibling(zp, xp, h):
        arrive(zp, xp, 1 - core, h)

    tall = 4 * width

    def product(zp, begin, depth, fresh=False, scaled=False):
        step = (zp - z + STEPS) % STEPS
        begin = pl.multiple_of(begin, rows)

        def body(i, carry):
            lines = pl.ds(pl.multiple_of(i * tall, tall), tall)
            value = jnp.dot(
                stack[lines, pl.ds(begin, depth)],
                got[zp, pl.ds(begin, depth), :],
                preferred_element_type=jnp.float32,
            )
            if not fresh:
                value = total[step, lines, :] + value
            if scaled:
                value = value * (flags[0, step].astype(jnp.float32) * factor)
            total[step, lines, :] = value
            return carry

        lax.fori_loop(0, lags * width // tall, body, 0)

    def emit(zp):
        step = (zp - z + STEPS) % STEPS
        copies = []
        for j in range(lags):
            copy = pltpu.make_async_copy(
                total.at[step, pl.ds(j * width, width), :],
                out.at[j, :, pl.ds(pl.multiple_of(step * width, width), width)],
                out_sem.at[step, j],
            )
            copy.start()
            copies.append(copy)
        return copies

    load = pltpu.make_async_copy(own, got.at[z, pl.ds(pl.multiple_of(m * slab, slab), slab), :], own_sem)
    load.start()

    barrier = pltpu.get_barrier_semaphore()
    for target, cond in ((sibling, None), (across, None), (up, z < last), (down, z > 0)):
        def greet(target=target):
            pl.semaphore_signal(barrier, inc=1, device_id=target, device_id_type=pl.DeviceIdType.MESH)
        if cond is None:
            greet()
        else:
            pl.when(cond)(greet)
    pl.semaphore_wait(barrier, jnp.where(mid, 4, 3))
    load.wait()

    for h in range(PIECES):
        sent.append(send(z > 0, 0, down, z, x, h))
        sent.append(send(z < last, 1, up, z, x, h))
        sent.append(send(None, 2, across, z, x, h))
        sent.append(send(None, 3, sibling, z, x, h))

    for h in range(PIECES):
        from_x(z, h)
        lend(h, end)
        from_z(1, h)

    for h in range(PIECES):
        from_sibling(z, x, h)
        from_sibling(z, other, h)

    part = 512

    def widen(i, carry):
        at = pl.ds(pl.multiple_of(i * part, part), part)
        wide[at, :] = got[z, at, :].astype(jnp.float32)
        return carry

    lax.fori_loop(0, length // part, widen, 0)
    wide[pl.ds(length, LAGS), :] = jnp.zeros((LAGS, width), jnp.float32)

    def shift(i, carry):
        begin = pl.multiple_of(i * part, part)
        base = wide[pl.ds(pl.multiple_of(begin + m * lags, 8), part + 8), :]
        for j in range(lags):
            moved = base[j:j + part, :].astype(jnp.bfloat16)
            stack[pl.ds(j * width, width), pl.ds(begin, part)] = moved.T
        return carry

    lax.fori_loop(0, length // part, shift, 0)

    half = 2 * slab
    from_z(2, 0)
    product(z, 0, half, fresh=True)
    product(z, half, half, scaled=True)
    written = emit(z)

    for h in range(1, PIECES):
        from_z(2, h)
    for h in range(PIECES // 2, PIECES):
        lend(h, mid)
    for h in range(PIECES // 2):
        from_x(near, h)
    for h in range(PIECES):
        from_sibling(near, x, h)
    product(near, x * half, half, fresh=True)
    for h in range(PIECES):
        from_sibling(middle, x, h)
    product(middle, x * half, half, fresh=True)

    from_z(3, 0)
    for h in range(PIECES):
        from_x(middle, h)
    for h in range(PIECES):
        from_sibling(middle, other, h)
    product(middle, other * half, half, scaled=True)
    written += emit(middle)

    for h in range(1, PIECES):
        from_z(3, h)
    for h in range(PIECES):
        from_sibling(far, x, h)
    product(far, x * half, half, fresh=True)

    early = PIECES // 2
    depth = early * rows
    mine = (2 * other + core) * slab
    theirs = (2 * other + 1 - core) * slab
    for h in range(early):
        from_sibling(near, other, h)
    product(near, mine, depth)
    product(near, theirs, depth)
    for h in range(early):
        from_x(far, h)
    product(far, mine, depth)
    for h in range(early):
        from_sibling(far, other, h)
    product(far, theirs, depth)
    for h in range(early, PIECES):
        from_x(near, h)
        from_x(far, h)
    product(near, mine + depth, depth)
    product(far, mine + depth, depth)
    for h in range(early, PIECES):
        from_sibling(near, other, h)
    product(near, theirs + depth, depth, scaled=True)
    written += emit(near)
    for h in range(early, PIECES):
        from_sibling(far, other, h)
    product(far, theirs + depth, depth, scaled=True)
    written += emit(far)

    for cond, copy in sent:
        if cond is None:
            copy.wait_send()
        else:
            pl.when(cond)(copy.wait_send)
    for copy in written:
        copy.wait()


def fused(samples, pair_mask):
    slab, width = samples.shape
    slabs = lax.axis_size("tm")
    lags = LAGS // slabs
    length = slab * slabs
    return pl.pallas_call(
        functools.partial(kernel, slab, width, lags),
        out_shape=jax.ShapeDtypeStruct((lags, width, STEPS * width), jnp.float32),
        in_specs=[
            pl.BlockSpec(memory_space=pltpu.SMEM),
            pl.BlockSpec(memory_space=pl.ANY),
        ],
        out_specs=pl.BlockSpec(memory_space=pl.ANY),
        scratch_shapes=[
            pltpu.VMEM((STEPS, length, width), samples.dtype),
            pltpu.VMEM((length + LAGS, width), jnp.float32),
            pltpu.VMEM((lags * width, length), samples.dtype),
            pltpu.VMEM((STEPS, lags * width, width), jnp.float32),
            pltpu.SemaphoreType.DMA,
            pltpu.SemaphoreType.DMA((STEPS, lags)),
            pltpu.SemaphoreType.DMA((4, STEPS, 2, PIECES)),
            pltpu.SemaphoreType.DMA((STEPS, slabs, PIECES)),
        ],
        compiler_params=pltpu.CompilerParams(
            collective_id=0, has_side_effects=True, vmem_limit_bytes=56 * 1024 * 1024
        ),
        cost_estimate=pl.CostEstimate(
            flops=2 * lags * width * STEPS * width * length,
            bytes_accessed=4 * lags * width * STEPS * width,
            transcendentals=0,
        ),
    )(pair_mask, samples)


def solution(mesh):
    placed = (P(("group", "tm"), "chan"), P(("group", "chan"), None))
    whole_cycle = mesh.shape["chan"] == STEPS and mesh.shape["tm"] == 4
    return jax.shard_map(
        fused if whole_cycle else shards,
        mesh=mesh,
        in_specs=placed,
        out_specs=P("tm", ("group", "chan"), None),
        check_vma=False,
    )
```

```python
import functools

import jax
import jax.numpy as jnp
from jax import lax
from jax.experimental import pallas as pl
from jax.experimental.pallas import tpu as pltpu
from jax.sharding import PartitionSpec as P

LAGS = 32
STEPS = 4
PIECES = 2


def from_behind(value, axis, steps):
    count = lax.axis_size(axis)
    pairs = [(source, (source + steps) % count) for source in range(count)]
    return lax.ppermute(value, axis, pairs)


def cycle_partners(block):
    partners = [block]
    moving = block
    for step in range(1, STEPS):
        moving = from_behind(moving, "chan", -1)
        partners.append(moving)
    return partners


def lagged_product(stacked, partner, flag, count, width):

    def compute():
        product = lax.dot_general(
            stacked, partner, (((0,), (0,)), ((), ())), preferred_element_type=jnp.float32
        )
        return product.reshape(count, width, width)

    def nothing():
        return jnp.zeros((count, width, width), jnp.float32)

    return lax.cond(flag > 0, compute, nothing)


def shards(samples, pair_mask):
    width = samples.shape[1]
    slabs = lax.axis_size("tm")
    lag_dev = LAGS // slabs
    flags = pair_mask[0]
    time_total = samples.shape[0] * slabs
    series = lax.all_gather(samples, "tm", axis=0, tiled=True)
    partners = cycle_partners(series)
    length = series.shape[0]
    first = lax.axis_index("tm") * lag_dev
    padded = jnp.concatenate([series, jnp.zeros((LAGS, width), series.dtype)], axis=0)
    stacked = jnp.concatenate(
        [lax.dynamic_slice_in_dim(padded, first + j, length, 0) for j in range(lag_dev)], axis=1
    )
    raw = jnp.concatenate(
        [
            lagged_product(stacked, partners[step], flags[step], lag_dev, width)
            for step in range(STEPS)
        ],
        axis=2,
    )
    return raw / jnp.sqrt(jnp.float32(time_total))


def kernel(slab, width, lags, flags, own, out, got, wide, stack,
           own_sem, send_sem, recv_sem):
    z = lax.axis_index("chan")
    m = lax.axis_index("tm")
    x, core = m // 2, m % 2
    other = 1 - x
    last = STEPS - 1
    end = (z == 0) | (z == last)
    mid = (z > 0) & (z < last)
    twin = z + 1 - 2 * (z % 2)
    sibling = {"tm": 2 * x + 1 - core}
    across = {"tm": 2 * other + core}
    up, down = {"chan": z + 1}, {"chan": z - 1}
    rows = slab // PIECES
    length = 4 * slab
    factor = 1.0 / (float(length) ** 0.5)
    high = z // 2
    low = z % 2
    near = 1 + low
    far = 3 * (1 - high)
    middle = 6 - z - near - far
    sent = []

    def home(zp, xp, plane, h, count=1):
        begin = pl.multiple_of((2 * xp + plane) * slab + h * rows, rows)
        return got.at[zp, pl.ds(begin, count * rows), :]

    def send(cond, way, target, zp, xp, h):
        piece = home(zp, xp, core, h)
        copy = pltpu.make_async_remote_copy(
            src_ref=piece,
            dst_ref=piece,
            send_sem=send_sem.at[way, zp, xp, h],
            recv_sem=recv_sem.at[zp, 2 * xp + core, h],
            device_id=target,
            device_id_type=pl.DeviceIdType.MESH,
        )
        if cond is None:
            copy.start()
        else:
            pl.when(cond)(copy.start)
        return cond, copy

    def arrive(zp, xp, plane, h):
        piece = home(zp, xp, plane, h)
        pltpu.make_async_copy(piece, piece, recv_sem.at[zp, 2 * xp + plane, h]).wait()

    def from_z(r, h):
        for d in (1, -1):
            zp = z + d * r
            here = (zp >= 0) & (zp <= last)
            zq = jnp.clip(zp, 0, last)

            @pl.when(here)
            def _():
                arrive(zq, x, core, h)

            onward = (z > 0) if d == 1 else (z < last)
            sent.append(send(here & onward, 0 if d == 1 else 1, down if d == 1 else up, zq, x, h))
            skip = (zp == twin) if h >= PIECES // 2 else ((zp == twin) & mid)
            sent.append(send(here & jnp.logical_not(skip), 2, across, zq, x, h))
            sent.append(send(here, 3, sibling, zq, x, h))

    def lend(h, cond):
        sent.append(send(cond & (low == 0), 1, up, z, other, h))
        sent.append(send(cond & (low == 1), 0, down, z, other, h))

    def from_x(zp, h):
        arrive(zp, other, core, h)
        sent.append(send(None, 3, sibling, zp, other, h))

    def from_sibling(zp, xp, h):
        arrive(zp, xp, 1 - core, h)

    group = 4
    tall = group * width

    def product(zp, begin, depth, fresh=False, scaled=False):
        step = (zp - z + STEPS) % STEPS
        begin = pl.multiple_of(begin, rows)
        columns = pl.ds(pl.multiple_of(step * width, width), width)

        def body(i, carry):
            lines = pl.ds(pl.multiple_of(i * tall, tall), tall)
            value = jnp.dot(
                stack[lines, pl.ds(begin, depth)],
                got[zp, pl.ds(begin, depth), :],
                preferred_element_type=jnp.float32,
            )
            value = value.reshape(group, width, width)
            place = (pl.ds(i * group, group), slice(None), columns)
            if not fresh:
                value = out[place] + value
            if scaled:
                value = value * (flags[0, step].astype(jnp.float32) * factor)
            out[place] = value
            return carry

        lax.fori_loop(0, lags // group, body, 0)

    load = pltpu.make_async_copy(own, got.at[z, pl.ds(pl.multiple_of(m * slab, slab), slab), :], own_sem)
    load.start()

    barrier = pltpu.get_barrier_semaphore()
    for target, cond in ((sibling, None), (across, None), (up, z < last), (down, z > 0)):
        def greet(target=target):
            pl.semaphore_signal(barrier, inc=1, device_id=target, device_id_type=pl.DeviceIdType.MESH)
        if cond is None:
            greet()
        else:
            pl.when(cond)(greet)
    pl.semaphore_wait(barrier, jnp.where(mid, 4, 3))
    load.wait()

    for h in range(PIECES):
        sent.append(send(z > 0, 0, down, z, x, h))
        sent.append(send(z < last, 1, up, z, x, h))
        sent.append(send(None, 2, across, z, x, h))
        sent.append(send(None, 3, sibling, z, x, h))

    for h in range(PIECES):
        from_x(z, h)
        lend(h, end)
        from_z(1, h)

    for h in range(PIECES):
        from_sibling(z, x, h)
        from_sibling(z, other, h)

    part = 512

    def widen(i, carry):
        at = pl.ds(pl.multiple_of(i * part, part), part)
        wide[at, :] = got[z, at, :].astype(jnp.float32)
        return carry

    lax.fori_loop(0, length // part, widen, 0)
    wide[pl.ds(length, LAGS), :] = jnp.zeros((LAGS, width), jnp.float32)

    def shift(i, carry):
        begin = pl.multiple_of(i * part, part)
        base = wide[pl.ds(pl.multiple_of(begin + m * lags, 8), part + 8), :]
        for j in range(lags):
            moved = base[j:j + part, :].astype(jnp.bfloat16)
            stack[pl.ds(j * width, width), pl.ds(begin, part)] = moved.T
        return carry

    lax.fori_loop(0, length // part, shift, 0)

    half = 2 * slab
    from_z(2, 0)
    product(z, 0, half, fresh=True)
    product(z, half, half, scaled=True)

    for h in range(1, PIECES):
        from_z(2, h)
    for h in range(PIECES // 2, PIECES):
        lend(h, mid)
    for h in range(PIECES // 2):
        from_x(near, h)
    for h in range(PIECES):
        from_sibling(near, x, h)
    product(near, x * half, half, fresh=True)
    for h in range(PIECES):
        from_sibling(middle, x, h)
    product(middle, x * half, half, fresh=True)

    from_z(3, 0)
    for h in range(PIECES):
        from_x(middle, h)
    for h in range(PIECES):
        from_sibling(middle, other, h)
    product(middle, other * half, half, scaled=True)

    for h in range(1, PIECES):
        from_z(3, h)
    for h in range(PIECES):
        from_sibling(far, x, h)
    product(far, x * half, half, fresh=True)

    early = PIECES // 2
    depth = early * rows
    mine = (2 * other + core) * slab
    theirs = (2 * other + 1 - core) * slab
    for h in range(early):
        from_sibling(near, other, h)
    product(near, mine, depth)
    product(near, theirs, depth)
    for h in range(early):
        from_x(far, h)
    product(far, mine, depth)
    for h in range(early):
        from_sibling(far, other, h)
    product(far, theirs, depth)
    for h in range(early, PIECES):
        from_x(near, h)
        from_x(far, h)
    product(near, mine + depth, depth)
    product(far, mine + depth, depth)
    for h in range(early, PIECES):
        from_sibling(near, other, h)
    product(near, theirs + depth, depth, scaled=True)
    for h in range(early, PIECES):
        from_sibling(far, other, h)
    product(far, theirs + depth, depth, scaled=True)

    for cond, copy in sent:
        if cond is None:
            copy.wait_send()
        else:
            pl.when(cond)(copy.wait_send)


def fused(samples, pair_mask):
    slab, width = samples.shape
    slabs = lax.axis_size("tm")
    lags = LAGS // slabs
    length = slab * slabs
    return pl.pallas_call(
        functools.partial(kernel, slab, width, lags),
        out_shape=pltpu.VMEM((lags, width, STEPS * width), jnp.float32),
        in_specs=[
            pl.BlockSpec(memory_space=pltpu.SMEM),
            pl.BlockSpec(memory_space=pl.ANY),
        ],
        out_specs=pl.BlockSpec(memory_space=pltpu.VMEM),
        scratch_shapes=[
            pltpu.VMEM((STEPS, length, width), samples.dtype),
            pltpu.VMEM((length + LAGS, width), jnp.float32),
            pltpu.VMEM((lags * width, length), samples.dtype),
            pltpu.SemaphoreType.DMA,
            pltpu.SemaphoreType.DMA((4, STEPS, 2, PIECES)),
            pltpu.SemaphoreType.DMA((STEPS, slabs, PIECES)),
        ],
        compiler_params=pltpu.CompilerParams(
            collective_id=0, has_side_effects=True, vmem_limit_bytes=48 * 1024 * 1024
        ),
        cost_estimate=pl.CostEstimate(
            flops=2 * lags * width * STEPS * width * length,
            bytes_accessed=4 * lags * width * STEPS * width,
            transcendentals=0,
        ),
    )(pair_mask, samples)


def solution(mesh):
    placed = (P(("group", "tm"), "chan"), P(("group", "chan"), None))
    whole_cycle = mesh.shape["chan"] == STEPS and mesh.shape["tm"] == 4
    return jax.shard_map(
        fused if whole_cycle else shards,
        mesh=mesh,
        in_specs=placed,
        out_specs=P("tm", ("group", "chan"), None),
        check_vma=False,
    )
```
